32 devices in a mesh: tok: 8 (over z, x), tp: 4 (over y, core).
Axes of the slice: x: 2, y: 2, z: 4, core: 2. Of those that a mesh axis runs over, the one named last changes fastest.
Arguments:
- tokens: bfloat16 [4096, 8192], P('tok', 'tp'), may hold values from -6 to 6
- frozen_weight: bfloat16 [8192, 2048], P('tp'), may hold values from -0.0625 to 0.0625
- adapter_down_matrices: bfloat16 [64, 8192, 64], P('tok', 'tp'), may hold values from -0.0625 to 0.0625
- adapter_up_matrices: bfloat16 [64, 64, 2048], P('tok', None, 'tp'), may hold values from -0.75 to 0.75
- adapter_per_block: int32 [256], P('tok'), may hold values from 0 to 63, as said below
- slot_per_adapter: int32 [64], replicated, may hold values from 0 to 63, as said below
- rank_per_adapter: int32 [64], replicated, may hold values from 16 to 64
- output_gradient: bfloat16 [4096, 2048], P('tok', 'tp'), may hold values from -6 to 6
Outputs:
- projected: bfloat16 [4096, 2048], P('tok', 'tp')
- token_gradient: bfloat16 [4096, 8192], P('tok', 'tp')
- grad_down: float32 [64, 8192, 64], P('tok', 'tp')
- grad_up: float32 [64, 64, 2048], P('tok', None, 'tp')
The draws below stay inside these ranges and needn't reach their ends.
Inputs may be any that keep to these rules, and one draw needn't show every extreme that they name: `adapter_per_block`: block b covers tokens b * 16 to (b + 1) * 16 - 1. Among the blocks of one index of tok, at most 8 have adapters stored on any one index of tok (slots k with k // 8 equal), and one index of tok receives exactly 8 such blocks from every index. A permutation: adapter a is stored in slot slot_per_adapter[a] of adapter_down_matrices and adapter_up_matrices.
All inputs are finite; a program needn't handle non-finite values.
Results may differ from the reference program's by a relative error of at most 0.0033.
Values may be sent and summed in bfloat16 or wider, within the bound.
A program may use at most 128 MiB of HBM per device.

```python
import jax
import jax.numpy as jnp
from jax import lax

MODEL_WIDTH = 8192
KEY_VALUE_WIDTH = 2048
MAX_RANK = 64
ALPHA = 32
BLOCK_TOKENS = 16
ADP_DEV = 8
ADAPTER_TOTAL = 64
TOKENS = 4096
BLOCKS = 256
CAP = 8


def joint_layout(key):
    owner_count = ADAPTER_TOTAL // ADP_DEV
    per_device = BLOCKS // owner_count
    storage = jax.random.permutation(jax.random.fold_in(key, 101), ADAPTER_TOTAL).astype(jnp.int32)
    popular = jax.random.randint(jax.random.fold_in(key, 102), (), 0, owner_count)
    tickets = jnp.arange(owner_count * CAP, dtype=jnp.int32)
    ticket_owner = tickets // CAP
    device_keys = jax.random.split(jax.random.fold_in(key, 103), owner_count)

    def one_device(device_key):
        first_key, second_key, third_key, fourth_key = jax.random.split(device_key, 4)
        shuffled = jax.random.permutation(first_key, owner_count * CAP).astype(jnp.int32)
        position = jnp.argsort(shuffled).astype(jnp.int32)
        priority = jnp.where(ticket_owner == popular, position - owner_count * CAP, position)
        chosen = jnp.argsort(priority)[:per_device].astype(jnp.int32)
        owner_seq = chosen // CAP
        owner_seq = owner_seq[jax.random.permutation(second_key, per_device)]
        local_pick = jnp.minimum(jax.random.randint(third_key, (per_device,), 0, ADP_DEV), jax.random.randint(fourth_key, (per_device,), 0, ADP_DEV))
        return (owner_seq * ADP_DEV + local_pick).astype(jnp.int32)
    slot_seq = jax.vmap(one_device)(device_keys).reshape(BLOCKS)
    inverse = jnp.argsort(storage).astype(jnp.int32)
    return (storage, inverse[slot_seq].astype(jnp.int32))


def draw_adapter_per_block(key, part):
    return joint_layout(key)[1]


def draw_slot_per_adapter(key, part):
    return joint_layout(key)[0]


def touch_ends(entries, stream_key, low, top_value):
    extent = entries.shape
    place = [jax.random.randint(jax.random.fold_in(stream_key, axis), (), 0, extent[axis]) for axis in range(len(extent))]
    entries = entries.at[tuple(place)].set(low)
    longest = extent.index(max(extent))
    place[longest] = (place[longest] + 1) % extent[longest]
    return entries.at[tuple(place)].set(top_value)


def level_of(rng, dims, pieces, smallest, high):
    loudness = 1.0
    for axis_at, blocks in pieces:
        steps = jax.random.uniform(jax.random.fold_in(jax.random.fold_in(rng, 6), axis_at), (blocks,), jnp.float32, smallest / len(pieces), high / len(pieces))
        loudness = loudness * jnp.repeat(jnp.exp(steps), dims[axis_at] // blocks).reshape((-1,) + (1,) * (len(dims) - 1 - axis_at))
    return loudness


def noise(stream_key, shape, deviation, bound, cuts=(), kind=jnp.bfloat16):
    array = jax.random.normal(stream_key, shape, jnp.float32) * deviation
    if len(cuts) > 0:
        array = level_of(stream_key, shape, cuts, -0.22, 0.18) * array
    return jnp.clip(array, min=-bound, max=bound).astype(kind)


def setup_inputs(seed: int = 0) -> dict:
    keys = jax.random.split(jax.random.key(seed), 9)
    return {
        "tokens": noise(keys[0], (TOKENS, MODEL_WIDTH), 1.0, 6.0, ((0, 8), (1, 4))),
        "frozen_weight": noise(keys[1], (MODEL_WIDTH, KEY_VALUE_WIDTH), MODEL_WIDTH ** -0.5, 0.0625, ((0, 4),)),
        "adapter_down_matrices": noise(keys[2], (ADAPTER_TOTAL, MODEL_WIDTH, MAX_RANK), MODEL_WIDTH ** -0.5, 0.0625, ((0, 8), (1, 4))),
        "adapter_up_matrices": noise(keys[3], (ADAPTER_TOTAL, MAX_RANK, KEY_VALUE_WIDTH), MAX_RANK ** -0.5, 0.75, ((0, 8), (2, 4))),
        "adapter_per_block": draw_adapter_per_block(jax.random.fold_in(keys[8], 71), 0),
        "slot_per_adapter": draw_slot_per_adapter(jax.random.fold_in(keys[8], 71), 0),
        "rank_per_adapter": touch_ends(jax.random.randint(keys[6], (ADAPTER_TOTAL,), MAX_RANK // 4, MAX_RANK + 1), jax.random.fold_in(keys[6], 1), MAX_RANK // 4, MAX_RANK).astype(jnp.int32),
        "output_gradient": noise(keys[7], (TOKENS, KEY_VALUE_WIDTH), 1.0, 6.0, ((0, 8), (1, 4))),
    }


def reference(tokens, frozen_weight, adapter_down_matrices, adapter_up_matrices, adapter_per_block, slot_per_adapter, rank_per_adapter, output_gradient):
    block_count = tokens.shape[0] // BLOCK_TOKENS
    slot_of = slot_per_adapter[adapter_per_block].astype(jnp.int32)
    rank_of = rank_per_adapter[adapter_per_block].astype(jnp.int32)
    scale_of = jnp.float32(ALPHA) / rank_of.astype(jnp.float32)
    keep_cols = jnp.arange(MAX_RANK, dtype=jnp.int32)[None, :] < rank_of[:, None]
    base_out = jnp.dot(tokens, frozen_weight, preferred_element_type=jnp.float32)
    frozen_input_gradient = lax.dot_general(output_gradient, frozen_weight, (((1,), (1,)), ((), ())), preferred_element_type=jnp.float32)
    tok_blocks = tokens.reshape(block_count, BLOCK_TOKENS, MODEL_WIDTH)
    grad_blocks = output_gradient.reshape(block_count, BLOCK_TOKENS, KEY_VALUE_WIDTH)

    def one_block(state_pair, block_item):
        down_matrix_sum, up_matrix_sum = state_pair
        storage_position, adapter_scale, keep, rows_in, grads_in = block_item
        down_matrix = lax.dynamic_index_in_dim(adapter_down_matrices, storage_position, 0, keepdims=False)
        up_matrix = lax.dynamic_index_in_dim(adapter_up_matrices, storage_position, 0, keepdims=False)
        reduced_rows = jnp.where(keep[None, :], jnp.dot(rows_in, down_matrix, preferred_element_type=jnp.float32), 0.0).astype(jnp.bfloat16)
        adapter_increment = adapter_scale * jnp.dot(reduced_rows, up_matrix, preferred_element_type=jnp.float32)
        pulled = lax.dot_general(grads_in, up_matrix, (((1,), (1,)), ((), ())), preferred_element_type=jnp.float32)
        reduced_gradient = (adapter_scale * jnp.where(keep[None, :], pulled, 0.0)).astype(jnp.bfloat16)
        adapter_input_gradient = lax.dot_general(reduced_gradient, down_matrix, (((1,), (1,)), ((), ())), preferred_element_type=jnp.float32)
        down_add = jnp.dot(rows_in.T, reduced_gradient, preferred_element_type=jnp.float32)
        up_add = adapter_scale * jnp.dot(reduced_rows.T, grads_in, preferred_element_type=jnp.float32)
        old_down = lax.dynamic_index_in_dim(down_matrix_sum, storage_position, 0, keepdims=False)
        old_up = lax.dynamic_index_in_dim(up_matrix_sum, storage_position, 0, keepdims=False)
        down_matrix_sum = lax.dynamic_update_index_in_dim(down_matrix_sum, old_down + down_add, storage_position, 0)
        up_matrix_sum = lax.dynamic_update_index_in_dim(up_matrix_sum, old_up + up_add, storage_position, 0)
        return (down_matrix_sum, up_matrix_sum), (adapter_increment, adapter_input_gradient)

    starting_offsets = (jnp.zeros(adapter_down_matrices.shape, jnp.float32), jnp.zeros(adapter_up_matrices.shape, jnp.float32))
    (grad_down, grad_up), (deltas, backs) = lax.scan(one_block, starting_offsets, (slot_of, scale_of, keep_cols, tok_blocks, grad_blocks))
    projected = (base_out + deltas.reshape(tokens.shape[0], KEY_VALUE_WIDTH)).astype(jnp.bfloat16)
    token_gradient = (frozen_input_gradient + backs.reshape(tokens.shape[0], MODEL_WIDTH)).astype(jnp.bfloat16)
    return projected, token_gradient, grad_down, grad_up
```

```python
import jax
import jax.numpy as jnp
from jax import lax
from jax.sharding import PartitionSpec as P

ALPHA = 32
BLOCK_TOKENS = 16


def exchange(rows, tok_count):
    total, width = rows.shape
    parts = rows.reshape(tok_count, total // tok_count, width)
    return lax.all_to_all(parts, "tok", split_axis=0, concat_axis=0, tiled=True).reshape(
        total, width
    )


def per_device(
    tokens,
    frozen_weight,
    adapter_down_matrices,
    adapter_up_matrices,
    adapter_per_block,
    slot_per_adapter,
    rank_per_adapter,
    output_gradient,
):
    tok_count = lax.axis_size("tok")
    token_rows = tokens.shape[0]
    block_count = adapter_per_block.shape[0]
    number_adapters, width_portion, rank_ceiling = adapter_down_matrices.shape
    capacity = max(2, 2 * block_count // tok_count)
    storage_position_count = tok_count * capacity
    row_total = storage_position_count * BLOCK_TOKENS
    adapter_total = slot_per_adapter.shape[0]
    stacked = number_adapters * rank_ceiling

    adapter_ids = jnp.arange(adapter_total, dtype=jnp.int32)
    matches = adapter_per_block[:, None] == adapter_ids[None, :]
    block_slot = jnp.sum(jnp.where(matches, slot_per_adapter[None, :], 0), axis=1)
    owner_ids = block_slot // number_adapters
    block_ids = jnp.arange(block_count, dtype=jnp.int32)
    earlier = (owner_ids[:, None] == owner_ids[None, :]) & (block_ids[None, :] < block_ids[:, None])
    position = jnp.sum(earlier.astype(jnp.int32), axis=1)
    destination = owner_ids * capacity + position
    within = jnp.arange(BLOCK_TOKENS, dtype=jnp.int32)
    target_row = (destination[:, None] * BLOCK_TOKENS + within[None, :]).reshape(token_rows)
    place = (jnp.arange(row_total, dtype=jnp.int32)[:, None] == target_row[None, :]).astype(
        jnp.bfloat16
    )
    send_grads = jnp.dot(place, output_gradient, preferred_element_type=jnp.float32).astype(
        jnp.bfloat16
    )
    gradient_rows = exchange(send_grads, tok_count)
    everyones = lax.all_gather(block_slot, "tok", axis=0, tiled=False)
    ours = everyones // number_adapters == lax.axis_index("tok")
    before = block_ids[None, :] < block_ids[:, None]
    rank_in_source = jnp.sum((ours[:, None, :] & before[None, :, :]).astype(jnp.int32), axis=2)
    in_slot = ours[:, None, :] & (
        rank_in_source[:, None, :] == jnp.arange(capacity, dtype=jnp.int32)[None, :, None]
    )
    arrived_adapter = (
        jnp.sum(jnp.where(in_slot, everyones[:, None, :] % number_adapters + 1, 0), axis=2) - 1
    ).reshape(storage_position_count)
    send_rows = jnp.dot(place, tokens, preferred_element_type=jnp.float32).astype(jnp.bfloat16)
    input_rows = exchange(send_rows, tok_count)

    base_out = lax.psum_scatter(
        lax.dot_general(
            frozen_weight, tokens, (((0,), (1,)), ((), ())), preferred_element_type=jnp.float32
        ),
        "tp",
        scatter_dimension=0,
        tiled=True,
    ).T
    frozen_input_gradient = lax.dot_general(
        lax.all_gather(output_gradient, "tp", axis=1, tiled=True),
        frozen_weight,
        (((1,), (1,)), ((), ())),
        preferred_element_type=jnp.float32,
    )

    chosen = arrived_adapter[:, None] == jnp.arange(number_adapters, dtype=jnp.int32)[None, :]
    chosen_rows = jnp.broadcast_to(
        chosen[:, None, :], (storage_position_count, BLOCK_TOKENS, number_adapters)
    ).reshape(row_total, number_adapters)
    chosen_float = chosen_rows.astype(jnp.float32)
    chosen_half = chosen_rows.astype(jnp.bfloat16)
    stored_ids = lax.axis_index("tok") * number_adapters + jnp.arange(
        number_adapters, dtype=jnp.int32
    )
    stored_match = slot_per_adapter[None, :] == stored_ids[:, None]
    stored_rank = jnp.sum(jnp.where(stored_match, rank_per_adapter[None, :], 0), axis=1)
    stored_scale = jnp.where(
        stored_rank > 0, jnp.float32(ALPHA) / jnp.maximum(stored_rank, 1).astype(jnp.float32), 0.0
    )
    row_rank = jnp.sum(jnp.where(chosen_rows, stored_rank[None, :], 0), axis=1)
    scale_per_row = jnp.sum(chosen_float * stored_scale[None, :], axis=1)
    keep_cols = jnp.arange(rank_ceiling, dtype=jnp.int32)[None, :] < row_rank[:, None]

    down_stack = adapter_down_matrices.transpose(0, 2, 1).reshape(stacked, width_portion)
    up_stack = adapter_up_matrices.reshape(stacked, adapter_up_matrices.shape[2])

    pull_all = lax.dot_general(
        gradient_rows, up_stack, (((1,), (1,)), ((), ())), preferred_element_type=jnp.float32
    ).reshape(row_total, number_adapters, rank_ceiling)
    pull_sum = lax.psum(jnp.sum(pull_all * chosen_float[:, :, None], axis=1), "tp")
    reduced_gradient = (scale_per_row[:, None] * jnp.where(keep_cols, pull_sum, 0.0)).astype(
        jnp.bfloat16
    )
    gradient_picked = (chosen_half[:, :, None] * reduced_gradient[:, None, :]).reshape(
        row_total, stacked
    )
    adapter_output_rows = jnp.dot(
        gradient_picked, down_stack, preferred_element_type=jnp.float32
    ).astype(jnp.bfloat16)
    adapter_output_rows, frozen_input_gradient = lax.optimization_barrier(
        (adapter_output_rows, frozen_input_gradient)
    )
    rows_back = exchange(adapter_output_rows, tok_count)

    low_all = lax.dot_general(
        input_rows, down_stack, (((1,), (1,)), ((), ())), preferred_element_type=jnp.float32
    ).reshape(row_total, number_adapters, rank_ceiling)
    low_sum = lax.psum(jnp.sum(low_all * chosen_float[:, :, None], axis=1), "tp")
    reduced_rows = jnp.where(keep_cols, low_sum, 0.0).astype(jnp.bfloat16)
    reduced_picked = (chosen_half[:, :, None] * reduced_rows[:, None, :]).reshape(
        row_total, stacked
    )
    adapter_increment = (
        scale_per_row[:, None]
        * jnp.dot(reduced_picked, up_stack, preferred_element_type=jnp.float32)
    ).astype(jnp.bfloat16)
    adapter_increment, rows_back = lax.optimization_barrier((adapter_increment, rows_back))
    delta_back = exchange(adapter_increment, tok_count)

    grad_down = jnp.einsum(
        "rd,rak->adk",
        input_rows,
        gradient_picked.reshape(row_total, number_adapters, rank_ceiling),
        preferred_element_type=jnp.float32,
    )
    grad_up = stored_scale[:, None, None] * lax.dot_general(
        reduced_picked, gradient_rows, (((0,), (0,)), ((), ())), preferred_element_type=jnp.float32
    ).reshape(adapter_up_matrices.shape)

    taken = (((0,), (0,)), ((), ()))
    token_gradient = (
        frozen_input_gradient
        + lax.dot_general(place, rows_back, taken, preferred_element_type=jnp.float32)
    ).astype(jnp.bfloat16)
    projected = (
        base_out + lax.dot_general(place, delta_back, taken, preferred_element_type=jnp.float32)
    ).astype(jnp.bfloat16)
    return (projected, token_gradient, grad_down, grad_up)


def solution(mesh):
    return jax.shard_map(
        per_device,
        mesh=mesh,
        in_specs=(
            P("tok", "tp"),
            P("tp", None),
            P("tok", "tp", None),
            P("tok", None, "tp"),
            P("tok"),
            P(),
            P(),
            P("tok", "tp"),
        ),
        out_specs=(P("tok", "tp"), P("tok", "tp"), P("tok", "tp", None), P("tok", None, "tp")),
        check_vma=False,
    )
```

```python
import jax
import jax.numpy as jnp
from jax import lax
from jax.sharding import PartitionSpec as P

ALPHA = 32
BLOCK_TOKENS = 16


def exchange(rows, tok_count):
    total, width = rows.shape
    parts = rows.reshape(tok_count, total // tok_count, width)
    return lax.all_to_all(parts, "tok", split_axis=0, concat_axis=0, tiled=True).reshape(
        total, width
    )


def per_device(
    tokens,
    frozen_weight,
    adapter_down_matrices,
    adapter_up_matrices,
    adapter_per_block,
    slot_per_adapter,
    rank_per_adapter,
    output_gradient,
):
    tok_count = lax.axis_size("tok")
    token_rows = tokens.shape[0]
    block_count = adapter_per_block.shape[0]
    number_adapters, width_portion, rank_ceiling = adapter_down_matrices.shape
    capacity = max(2, 2 * block_count // tok_count)
    storage_position_count = tok_count * capacity
    row_total = storage_position_count * BLOCK_TOKENS
    adapter_total = slot_per_adapter.shape[0]
    stacked = number_adapters * rank_ceiling

    adapter_ids = jnp.arange(adapter_total, dtype=jnp.int32)
    matches = adapter_per_block[:, None] == adapter_ids[None, :]
    block_slot = jnp.sum(jnp.where(matches, slot_per_adapter[None, :], 0), axis=1)
    owner_ids = block_slot // number_adapters
    local_index = block_slot % number_adapters
    block_ids = jnp.arange(block_count, dtype=jnp.int32)
    earlier = (owner_ids[:, None] == owner_ids[None, :]) & (block_ids[None, :] < block_ids[:, None])
    position = jnp.sum(earlier.astype(jnp.int32), axis=1)
    destination = owner_ids * capacity + position
    within = jnp.arange(BLOCK_TOKENS, dtype=jnp.int32)
    target_row = (destination[:, None] * BLOCK_TOKENS + within[None, :]).reshape(token_rows)
    place = (jnp.arange(row_total, dtype=jnp.int32)[:, None] == target_row[None, :]).astype(
        jnp.bfloat16
    )
    part_rows = capacity * BLOCK_TOKENS
    long_rows = part_rows + BLOCK_TOKENS
    column_portion = output_gradient.shape[1]
    long_target = (
        (owner_ids * long_rows + position * BLOCK_TOKENS)[:, None] + within[None, :]
    ).reshape(token_rows)
    note_target = owner_ids * long_rows + part_rows
    notes = jnp.where(
        position[:, None] == jnp.arange(column_portion, dtype=jnp.int32)[None, :],
        (local_index + 1)[:, None],
        0,
    ).astype(jnp.bfloat16)
    place_long = (
        jnp.arange(tok_count * long_rows, dtype=jnp.int32)[:, None]
        == jnp.concatenate([long_target, note_target])[None, :]
    ).astype(jnp.bfloat16)
    send_grads = jnp.dot(
        place_long,
        jnp.concatenate([output_gradient, notes], axis=0),
        preferred_element_type=jnp.float32,
    ).astype(jnp.bfloat16)
    arrived = exchange(send_grads, tok_count).reshape(tok_count, long_rows, column_portion)
    gradient_rows = arrived[:, :part_rows, :].reshape(row_total, column_portion)
    arrived_adapter = (
        arrived[:, part_rows, :capacity].astype(jnp.int32).reshape(storage_position_count) - 1
    )
    send_rows = jnp.dot(place, tokens, preferred_element_type=jnp.float32).astype(jnp.bfloat16)
    input_rows = exchange(send_rows, tok_count)

    base_out = lax.psum_scatter(
        lax.dot_general(
            frozen_weight, tokens, (((0,), (1,)), ((), ())), preferred_element_type=jnp.float32
        ),
        "tp",
        scatter_dimension=0,
        tiled=True,
    ).T
    frozen_input_gradient = lax.dot_general(
        lax.all_gather(output_gradient, "tp", axis=1, tiled=True),
        frozen_weight,
        (((1,), (1,)), ((), ())),
        preferred_element_type=jnp.float32,
    )

    chosen = arrived_adapter[:, None] == jnp.arange(number_adapters, dtype=jnp.int32)[None, :]
    chosen_rows = jnp.broadcast_to(
        chosen[:, None, :], (storage_position_count, BLOCK_TOKENS, number_adapters)
    ).reshape(row_total, number_adapters)
    chosen_float = chosen_rows.astype(jnp.float32)
    chosen_half = chosen_rows.astype(jnp.bfloat16)
    stored_ids = lax.axis_index("tok") * number_adapters + jnp.arange(
        number_adapters, dtype=jnp.int32
    )
    stored_match = slot_per_adapter[None, :] == stored_ids[:, None]
    stored_rank = jnp.sum(jnp.where(stored_match, rank_per_adapter[None, :], 0), axis=1)
    stored_scale = jnp.where(
        stored_rank > 0, jnp.float32(ALPHA) / jnp.maximum(stored_rank, 1).astype(jnp.float32), 0.0
    )
    row_rank = jnp.sum(jnp.where(chosen_rows, stored_rank[None, :], 0), axis=1)
    scale_per_row = jnp.sum(chosen_float * stored_scale[None, :], axis=1)
    keep_cols = jnp.arange(rank_ceiling, dtype=jnp.int32)[None, :] < row_rank[:, None]

    down_stack = adapter_down_matrices.transpose(0, 2, 1).reshape(stacked, width_portion)
    up_stack = adapter_up_matrices.reshape(stacked, adapter_up_matrices.shape[2])

    pull_all = lax.dot_general(
        gradient_rows, up_stack, (((1,), (1,)), ((), ())), preferred_element_type=jnp.float32
    ).reshape(row_total, number_adapters, rank_ceiling)
    pull_sum = lax.psum(jnp.sum(pull_all * chosen_float[:, :, None], axis=1), "tp")
    reduced_gradient = (scale_per_row[:, None] * jnp.where(keep_cols, pull_sum, 0.0)).astype(
        jnp.bfloat16
    )
    gradient_picked = (chosen_half[:, :, None] * reduced_gradient[:, None, :]).reshape(
        row_total, stacked
    )
    adapter_output_rows = jnp.dot(
        gradient_picked, down_stack, preferred_element_type=jnp.float32
    ).astype(jnp.bfloat16)
    adapter_output_rows, frozen_input_gradient = lax.optimization_barrier(
        (adapter_output_rows, frozen_input_gradient)
    )
    rows_back = exchange(adapter_output_rows, tok_count)

    low_all = lax.dot_general(
        input_rows, down_stack, (((1,), (1,)), ((), ())), preferred_element_type=jnp.float32
    ).reshape(row_total, number_adapters, rank_ceiling)
    low_sum = lax.psum(jnp.sum(low_all * chosen_float[:, :, None], axis=1), "tp")
    reduced_rows = jnp.where(keep_cols, low_sum, 0.0).astype(jnp.bfloat16)
    reduced_picked = (chosen_half[:, :, None] * reduced_rows[:, None, :]).reshape(
        row_total, stacked
    )
    adapter_increment = (
        scale_per_row[:, None]
        * jnp.dot(reduced_picked, up_stack, preferred_element_type=jnp.float32)
    ).astype(jnp.bfloat16)
    adapter_increment, rows_back = lax.optimization_barrier((adapter_increment, rows_back))
    delta_back = exchange(adapter_increment, tok_count)

    grad_down = jnp.einsum(
        "rd,rak->adk",
        input_rows,
        gradient_picked.reshape(row_total, number_adapters, rank_ceiling),
        preferred_element_type=jnp.float32,
    )
    grad_up = stored_scale[:, None, None] * lax.dot_general(
        reduced_picked, gradient_rows, (((0,), (0,)), ((), ())), preferred_element_type=jnp.float32
    ).reshape(adapter_up_matrices.shape)

    taken = (((0,), (0,)), ((), ()))
    token_gradient = (
        frozen_input_gradient
        + lax.dot_general(place, rows_back, taken, preferred_element_type=jnp.float32)
    ).astype(jnp.bfloat16)
    projected = (
        base_out + lax.dot_general(place, delta_back, taken, preferred_element_type=jnp.float32)
    ).astype(jnp.bfloat16)
    return (projected, token_gradient, grad_down, grad_up)


def solution(mesh):
    return jax.shard_map(
        per_device,
        mesh=mesh,
        in_specs=(
            P("tok", "tp"),
            P("tp", None),
            P("tok", "tp", None),
            P("tok", None, "tp"),
            P("tok"),
            P(),
            P(),
            P("tok", "tp"),
        ),
        out_specs=(P("tok", "tp"), P("tok", "tp"), P("tok", "tp", None), P("tok", None, "tp")),
        check_vma=False,
    )
```

```python
import jax
import jax.numpy as jnp
from jax import lax
from jax.sharding import PartitionSpec as P

ALPHA = 32
BLOCK_TOKENS = 16


def exchange(rows, tok_count):
    total, width = rows.shape
    parts = rows.reshape(tok_count, total // tok_count, width)
    return lax.all_to_all(parts, "tok", split_axis=0, concat_axis=0, tiled=True).reshape(
        total, width
    )


def per_device(
    tokens,
    frozen_weight,
    adapter_down_matrices,
    adapter_up_matrices,
    adapter_per_block,
    slot_per_adapter,
    rank_per_adapter,
    output_gradient,
):
    tok_count = lax.axis_size("tok")
    token_rows = tokens.shape[0]
    block_count = adapter_per_block.shape[0]
    number_adapters, width_portion, rank_ceiling = adapter_down_matrices.shape
    capacity = max(2, 2 * block_count // tok_count)
    storage_position_count = tok_count * capacity
    row_total = storage_position_count * BLOCK_TOKENS
    adapter_total = slot_per_adapter.shape[0]
    stacked = number_adapters * rank_ceiling

    adapter_ids = jnp.arange(adapter_total, dtype=jnp.int32)
    matches = adapter_per_block[:, None] == adapter_ids[None, :]
    block_slot = jnp.sum(jnp.where(matches, slot_per_adapter[None, :], 0), axis=1)
    owner_ids = block_slot // number_adapters
    local_index = block_slot % number_adapters
    block_ids = jnp.arange(block_count, dtype=jnp.int32)
    earlier = (owner_ids[:, None] == owner_ids[None, :]) & (block_ids[None, :] < block_ids[:, None])
    position = jnp.sum(earlier.astype(jnp.int32), axis=1)
    destination = owner_ids * capacity + position
    within = jnp.arange(BLOCK_TOKENS, dtype=jnp.int32)
    target_row = (destination[:, None] * BLOCK_TOKENS + within[None, :]).reshape(token_rows)
    place = (jnp.arange(row_total, dtype=jnp.int32)[:, None] == target_row[None, :]).astype(
        jnp.bfloat16
    )
    part_rows = capacity * BLOCK_TOKENS
    long_rows = part_rows + BLOCK_TOKENS
    column_portion = output_gradient.shape[1]
    long_target = (
        (owner_ids * long_rows + position * BLOCK_TOKENS)[:, None] + within[None, :]
    ).reshape(token_rows)
    note_target = owner_ids * long_rows + part_rows
    notes = jnp.where(
        position[:, None] == jnp.arange(column_portion, dtype=jnp.int32)[None, :],
        (local_index + 1)[:, None],
        0,
    ).astype(jnp.bfloat16)
    place_long = (
        jnp.arange(tok_count * long_rows, dtype=jnp.int32)[:, None]
        == jnp.concatenate([long_target, note_target])[None, :]
    ).astype(jnp.bfloat16)
    send_grads = jnp.dot(
        place_long,
        jnp.concatenate([output_gradient, notes], axis=0),
        preferred_element_type=jnp.float32,
    ).astype(jnp.bfloat16)
    arrived = exchange(send_grads, tok_count).reshape(tok_count, long_rows, column_portion)
    gradient_rows = arrived[:, :part_rows, :].reshape(row_total, column_portion)
    arrived_adapter = (
        arrived[:, part_rows, :capacity].astype(jnp.int32).reshape(storage_position_count) - 1
    )
    send_rows = jnp.dot(place, tokens, preferred_element_type=jnp.float32).astype(jnp.bfloat16)
    input_rows = exchange(send_rows, tok_count)

    base_out = lax.psum_scatter(
        jnp.dot(tokens, frozen_weight, preferred_element_type=jnp.float32),
        "tp",
        scatter_dimension=1,
        tiled=True,
    )
    frozen_input_gradient = lax.dot_general(
        lax.all_gather(output_gradient, "tp", axis=1, tiled=True),
        frozen_weight,
        (((1,), (1,)), ((), ())),
        preferred_element_type=jnp.float32,
    )

    chosen = arrived_adapter[:, None] == jnp.arange(number_adapters, dtype=jnp.int32)[None, :]
    chosen_rows = jnp.broadcast_to(
        chosen[:, None, :], (storage_position_count, BLOCK_TOKENS, number_adapters)
    ).reshape(row_total, number_adapters)
    chosen_float = chosen_rows.astype(jnp.float32)
    chosen_half = chosen_rows.astype(jnp.bfloat16)
    stored_ids = lax.axis_index("tok") * number_adapters + jnp.arange(
        number_adapters, dtype=jnp.int32
    )
    stored_match = slot_per_adapter[None, :] == stored_ids[:, None]
    stored_rank = jnp.sum(jnp.where(stored_match, rank_per_adapter[None, :], 0), axis=1)
    stored_scale = jnp.where(
        stored_rank > 0, jnp.float32(ALPHA) / jnp.maximum(stored_rank, 1).astype(jnp.float32), 0.0
    )
    row_rank = jnp.sum(jnp.where(chosen_rows, stored_rank[None, :], 0), axis=1)
    scale_per_row = jnp.sum(chosen_float * stored_scale[None, :], axis=1)
    keep_cols = jnp.arange(rank_ceiling, dtype=jnp.int32)[None, :] < row_rank[:, None]

    down_stack = adapter_down_matrices.transpose(0, 2, 1).reshape(stacked, width_portion)
    up_stack = adapter_up_matrices.reshape(stacked, adapter_up_matrices.shape[2])

    pull_all = lax.dot_general(
        gradient_rows, up_stack, (((1,), (1,)), ((), ())), preferred_element_type=jnp.float32
    ).reshape(row_total, number_adapters, rank_ceiling)
    pull_sum = lax.psum(jnp.sum(pull_all * chosen_float[:, :, None], axis=1), "tp")
    reduced_gradient = (scale_per_row[:, None] * jnp.where(keep_cols, pull_sum, 0.0)).astype(
        jnp.bfloat16
    )
    gradient_picked = (chosen_half[:, :, None] * reduced_gradient[:, None, :]).reshape(
        row_total, stacked
    )
    adapter_output_rows = jnp.dot(
        gradient_picked, down_stack, preferred_element_type=jnp.float32
    ).astype(jnp.bfloat16)
    adapter_output_rows, frozen_input_gradient = lax.optimization_barrier(
        (adapter_output_rows, frozen_input_gradient)
    )
    rows_back = exchange(adapter_output_rows, tok_count)

    low_all = lax.dot_general(
        input_rows, down_stack, (((1,), (1,)), ((), ())), preferred_element_type=jnp.float32
    ).reshape(row_total, number_adapters, rank_ceiling)
    low_sum = lax.psum(jnp.sum(low_all * chosen_float[:, :, None], axis=1), "tp")
    reduced_rows = jnp.where(keep_cols, low_sum, 0.0).astype(jnp.bfloat16)
    reduced_picked = (chosen_half[:, :, None] * reduced_rows[:, None, :]).reshape(
        row_total, stacked
    )
    adapter_increment = (
        scale_per_row[:, None]
        * jnp.dot(reduced_picked, up_stack, preferred_element_type=jnp.float32)
    ).astype(jnp.bfloat16)
    adapter_increment, rows_back = lax.optimization_barrier((adapter_increment, rows_back))
    delta_back = exchange(adapter_increment, tok_count)

    grad_down = jnp.einsum(
        "rd,rak->adk",
        input_rows,
        gradient_picked.reshape(row_total, number_adapters, rank_ceiling),
        preferred_element_type=jnp.float32,
    )
    grad_up = stored_scale[:, None, None] * lax.dot_general(
        reduced_picked, gradient_rows, (((0,), (0,)), ((), ())), preferred_element_type=jnp.float32
    ).reshape(adapter_up_matrices.shape)

    taken = (((0,), (0,)), ((), ()))
    token_gradient = (
        frozen_input_gradient
        + lax.dot_general(place, rows_back, taken, preferred_element_type=jnp.float32)
    ).astype(jnp.bfloat16)
    projected = (
        base_out + lax.dot_general(place, delta_back, taken, preferred_element_type=jnp.float32)
    ).astype(jnp.bfloat16)
    return (projected, token_gradient, grad_down, grad_up)


def solution(mesh):
    return jax.shard_map(
        per_device,
        mesh=mesh,
        in_specs=(
            P("tok", "tp"),
            P("tp", None),
            P("tok", "tp", None),
            P("tok", None, "tp"),
            P("tok"),
            P(),
            P(),
            P("tok", "tp"),
        ),
        out_specs=(P("tok", "tp"), P("tok", "tp"), P("tok", "tp", None), P("tok", None, "tp")),
        check_vma=False,
    )
```
